768 devices in a mesh: row: 96 (over x, z, core), col: 8 (over y).
Axes of the slice: x: 4, y: 8, z: 12, core: 2. Of those that a mesh axis runs over, the one named last changes fastest.
Arguments:
- features: float32 [49152, 128], P(('row', 'col')), may hold values from -6 to 6
- tile_coords: int32 [96, 8, 54, 2], P('row', 'col'), may hold values from 0 to 47, as said below
- tile_count: int32 [96, 8], P('row', 'col'), may hold values from 13 to 54, as said below
- tile_values: bfloat16 [96, 8, 54, 128, 128], P('row', 'col'), may hold values from -0.078125 to 0.078125
- w_first: float32 [128, 128], replicated, may hold values from -0.5 to 0.5
- bias_first: float32 [128], replicated, may hold values from -3 to 3
- w_second: float32 [128, 128], replicated, may hold values from -0.5 to 0.5
- bias_second: float32 [128], replicated, may hold values from -3 to 3
Outputs:
- node_out: float32 [49152, 128], P(('row', 'col'))
The draws below stay inside these ranges and needn't reach their ends.
Inputs may be any that keep to these rules, and one draw needn't show every extreme that they name: `tile_coords`: each slot holds a tile row below 4 and a tile column below 48; the 54 pairs of one device are distinct. The first tile_count slots of a device are in use; some device uses all 54.
All inputs are finite; a program needn't handle non-finite values.
Results may differ from the reference program's by a relative error of at most 0.0034.
Values may be sent and summed in bfloat16 or wider, within the bound.
A program may use at most 32 MiB of HBM per device.

```python
import jax
import jax.numpy as jnp
from jax import lax

F = 128
HID = 128
TILE = 128
NODE_DEV = 64
RT = 4
CT = 48
SLOTS = 54
NODES = 49152
N_ROW = 96
N_COL = 8


def draw_tile_coords(key, part):
    key = jax.random.fold_in(key, 11)
    dev_keys = jax.random.split(key, N_ROW * N_COL)

    def one_device(dev_key):
        picked = jax.random.permutation(dev_key, RT * CT)[:SLOTS]
        return jnp.stack([picked // CT, picked % CT], axis=-1)
    return jax.vmap(one_device)(dev_keys).reshape(N_ROW, N_COL, SLOTS, 2).astype(jnp.int32)


def draw_tile_count(key, part):
    key = jax.random.fold_in(key, 23)
    first_key, second_key = jax.random.split(key)
    least_used = max(1, SLOTS // 4)
    counts = jax.random.randint(first_key, (N_ROW * N_COL,), least_used, SLOTS + 1)
    fullest = jax.random.randint(second_key, (), 0, N_ROW * N_COL)
    counts = jnp.where(jnp.arange(N_ROW * N_COL) == fullest, SLOTS, counts)
    return counts.reshape(N_ROW, N_COL).astype(jnp.int32)


def block_levels(own_key, shape, cuts, smallest, largest):
    gain, own = 1.0, jax.random.fold_in(own_key, 6)
    for axis_at, blocks in cuts:
        draws = jnp.exp(jax.random.uniform(jax.random.fold_in(own, axis_at), (blocks,), jnp.float32, smallest / len(cuts), largest / len(cuts)))
        gain = gain * jnp.repeat(draws, shape[axis_at] // blocks).reshape([-1 if axis == axis_at else 1 for axis in range(len(shape))])
    return gain


def noise(stream_key, dims, scale, bound, pieces=(), held_as=jnp.bfloat16):
    drawn = scale * jax.random.normal(stream_key, dims, jnp.float32)
    if pieces:
        drawn = drawn * block_levels(stream_key, dims, pieces, -0.22, 0.18)
    return jnp.clip(drawn, -bound, bound).astype(held_as)


def setup_inputs(seed: int = 0) -> dict:
    streams_of = jax.random.split(jax.random.key(seed), 9)
    return {
        "features": noise(streams_of[0], (NODES, F), 1.0, 6.0, ((0, 768),), jnp.float32),
        "tile_coords": draw_tile_coords(jax.random.fold_in(streams_of[8], 71), 0),
        "tile_count": draw_tile_count(jax.random.fold_in(streams_of[8], 71), 0),
        "tile_values": noise(streams_of[3], (N_ROW, N_COL, SLOTS, TILE, TILE), (SLOTS * TILE * N_COL // (2 * RT)) ** -0.5, 0.078125, ((0, 96), (1, 8))),
        "w_first": noise(streams_of[4], (F, HID), F ** -0.5, 0.5, (), jnp.float32),
        "bias_first": noise(streams_of[5], (HID,), 0.5, 3.0, (), jnp.float32),
        "w_second": noise(streams_of[6], (HID, HID), HID ** -0.5, 0.5, (), jnp.float32),
        "bias_second": noise(streams_of[7], (HID,), 0.5, 3.0, (), jnp.float32),
    }


def aggregate(node_rows, weight, tile_coords, tile_count, tile_values):
    mixed = jnp.dot(node_rows, weight, precision=lax.Precision.HIGHEST, preferred_element_type=jnp.float32).astype(jnp.bfloat16)
    columns = mixed.reshape(N_ROW, N_COL, NODE_DEV, HID).transpose(1, 0, 2, 3).reshape(N_COL, CT, TILE, HID)
    slot_index = jnp.arange(SLOTS, dtype=jnp.int32)
    tile_index = jnp.arange(RT, dtype=jnp.int32)

    def one_device(column_tiles, dev_coords, dev_values, dev_count):
        picked = jnp.take(column_tiles, dev_coords[:, 1], axis=0).astype(jnp.float32)
        products = jnp.einsum("kab,kbf->kaf", dev_values.astype(jnp.float32), picked, precision=lax.Precision.HIGHEST)
        chosen = ((dev_coords[:, 0][None, :] == tile_index[:, None]) & (slot_index < dev_count)[None, :]).astype(jnp.float32)
        return jnp.einsum("rk,kaf->raf", chosen, products, precision=lax.Precision.HIGHEST)

    def one_row(block_row):
        terms = jax.vmap(one_device)(columns, tile_coords[block_row], tile_values[block_row], tile_count[block_row])
        return jnp.sum(terms, axis=0).reshape(RT * TILE, HID)

    return lax.map(one_row, jnp.arange(N_ROW, dtype=jnp.int32)).reshape(NODES, HID)


def reference(features, tile_coords, tile_count, tile_values, w_first, bias_first, w_second, bias_second):
    agg_first = aggregate(features, w_first, tile_coords, tile_count, tile_values)
    h_first = jnp.maximum(agg_first + bias_first, 0.0)
    agg_second = aggregate(h_first, w_second, tile_coords, tile_count, tile_values)
    return agg_second + bias_second
```

```python
import functools

import jax
import jax.numpy as jnp
from jax import lax
from jax.experimental import pallas as pl
from jax.experimental.pallas import tpu as pltpu
from jax.sharding import PartitionSpec as P

MESH = pl.DeviceIdType.MESH
NX, NZ, NY = 4, 12, 8
TILE, RT, SLOTS = 128, 4, 54
FAR_Z = (6, 5, -5, 4, -4, 3, -3, 2, -2, 1, -1)
FAR_X = (2, 1, -1)
FAR_Y = (4, 3, -3, 2, -2, 1, -1)


def kernel(
    slot_ref, feat_ref, tiles_hbm, w1_ref, b1_ref, w2_ref, b2_ref, out_ref,
    tiles, half, zb, acc, part1, part2, back2, tile_sem,
    half_send, half_recv, z_send, z_recv, x_send, x_recv, c_send, c_recv,
    r1_send, r1_recv, r2_send, r2_recv,
):
    row, col = lax.axis_index("row"), lax.axis_index("col")
    core = row % 2
    chip = row // 2
    z, x = chip % NZ, chip // NZ

    def at(dx, dz, c, dy=0):
        return (
            (((x + dx + NX) % NX) * NZ + (z + dz + NZ) % NZ) * 2 + c,
            (col + dy + NY) % NY,
        )

    def remote(src, dst, send, recv, to):
        return pltpu.make_async_remote_copy(
            src_ref=src, dst_ref=dst, send_sem=send, recv_sem=recv, device_id=to, device_id_type=MESH
        )

    def step_dz(t):
        return (((t + 1) // 2) * (2 * (t % 2) - 1) + NZ) % NZ

    load = pltpu.make_async_copy(tiles_hbm, tiles.at[pl.ds(0, SLOTS)], tile_sem)
    load.start()

    barrier = pltpu.get_barrier_semaphore()

    def signal(to):
        pl.semaphore_signal(barrier, inc=1, device_id=to, device_id_type=MESH)

    sibling = at(0, 0, 1 - core)
    signal(sibling)
    for d in FAR_Y:
        signal(at(0, 0, 0, d))

    @pl.when(core == 1)
    def _():
        for d in FAR_Z:
            signal(at(0, d, 1))
        for d in FAR_X:
            signal(at(d, 0, 1))
        for d in FAR_Y:
            signal(at(0, 0, 1, d))

    tiles[SLOTS] = jnp.zeros((TILE, TILE), jnp.bfloat16)
    mixed = jnp.dot(
        feat_ref[...], w1_ref[...], precision=lax.Precision.HIGHEST, preferred_element_type=jnp.float32
    ).astype(jnp.bfloat16)

    def half_copy():
        return remote(half, zb.at[0, 0, 0, pl.ds(0, 64)], half_send, half_recv, sibling)

    @pl.when(core == 0)
    def _():
        half[...] = mixed
        pl.semaphore_wait(barrier, 1 + 7 + 7)
        half_copy().start()

    @pl.when(core == 1)
    def _():
        zb[0, 0, 0, 64:128] = mixed
        pl.semaphore_wait(barrier, 1 + 7 + 11 + 3)
        half_copy().wait_recv()

    def z_copy(layer, i):
        d = FAR_Z[i]
        return remote(
            zb.at[layer, 0, 0], zb.at[layer, -d % NZ, 0],
            z_send.at[layer, i], z_recv.at[layer, -d % NZ], at(0, d, 1),
        )

    def x_copy(layer, dz, i):
        d = FAR_X[i]
        return remote(
            zb.at[layer, dz, 0], zb.at[layer, dz, -d % NX],
            x_send.at[layer, dz, i], x_recv.at[layer, dz], at(d, 0, 1),
        )

    def c_copy(layer, dz, first, size, i):
        block = zb.at[layer, dz, pl.ds(first, size)]
        return remote(block, block, c_send.at[layer, dz, i], c_recv.at[layer, dz], sibling)

    def multiply(layer, dz):
        za = (z + dz) % NZ
        places = [((x + dx) % NX) * NZ + za for dx in range(NX)]
        lhs = jnp.concatenate(
            [
                jnp.concatenate([tiles[slot_ref[r * NX * NZ + p]] for p in places], axis=1)
                for r in range(RT)
            ],
            axis=0,
        )
        rhs = zb[layer, dz].reshape(NX * TILE, TILE)
        acc[layer] += jnp.dot(lhs, rhs, preferred_element_type=jnp.float32).reshape(NY, 64, TILE)

    def gather_multiply(layer):
        acc[layer] = jnp.zeros((NY, 64, TILE), jnp.float32)

        @pl.when(core == 1)
        def _():
            for i in range(len(FAR_Z)):
                z_copy(layer, i).start()
            for i in range(len(FAR_X)):
                x_copy(layer, 0, i).start()
            c_copy(layer, 0, 0, 1, 0).start()

            @pl.loop(1, NZ)
            def _(t):
                dz = step_dz(t)
                remote(
                    zb.at[layer, dz, 0], zb.at[layer, dz, 0], z_send.at[layer, 0], z_recv.at[layer, dz], sibling
                ).wait_recv()
                for i in range(len(FAR_X)):
                    x_copy(layer, dz, i).start()
                c_copy(layer, dz, 0, 1, 0).start()

            if layer == 0:
                load.wait()

            @pl.loop(0, NZ)
            def _(t):
                dz = step_dz(t)
                rest = zb.at[layer, dz, pl.ds(1, NX - 1)]
                remote(rest, rest, c_send.at[layer, dz, 1], x_recv.at[layer, dz], sibling).wait_recv()
                c_copy(layer, dz, 1, NX - 1, 1).start()
                multiply(layer, dz)

        @pl.when(core == 0)
        def _():
            if layer == 0:
                load.wait()

            @pl.loop(0, NZ)
            def _(t):
                dz = step_dz(t)
                c_copy(layer, dz, 0, NX, 0).wait_recv()
                multiply(layer, dz)

    gather_multiply(0)

    def r1_copy(i):
        d = FAR_Y[i]
        return remote(
            acc.at[0, (col + d + NY) % NY], part1.at[core, -d % NY], r1_send.at[i], r1_recv.at[core], at(0, 0, 1, d)
        )

    def r1_own():
        return remote(acc.at[0, col], part1.at[0, 0], r1_send.at[7], r1_recv.at[0], sibling)

    for i in range(len(FAR_Y)):
        r1_copy(i).start()

    @pl.when(core == 0)
    def _():
        r1_own().start()

    @pl.when(core == 1)
    def _():
        part1[1, 0] = acc[0, col]
        rest = part1.at[0]
        remote(rest, rest, r1_send.at[7], r1_recv.at[0], sibling).wait_recv()
        rest = part1.at[1, pl.ds(1, 7)]
        remote(rest, rest, r1_send.at[7], r1_recv.at[1], sibling).wait_recv()
        summed = jnp.sum(part1[...], axis=1).reshape(TILE, TILE)
        hidden = jnp.maximum(summed + b1_ref[...], 0.0)
        zb[1, 0, 0] = jnp.dot(
            hidden, w2_ref[...], precision=lax.Precision.HIGHEST, preferred_element_type=jnp.float32
        ).astype(jnp.bfloat16)

    gather_multiply(1)
    part2[...] = acc[1].astype(jnp.bfloat16)

    def r2_copy(i):
        d = FAR_Y[i]
        return remote(
            part2.at[(col + d + NY) % NY], back2.at[-d % NY - 1], r2_send.at[i], r2_recv, at(0, 0, core, d)
        )

    for i in range(len(FAR_Y)):
        r2_copy(i).start()
    remote(back2, back2, r2_send.at[0], r2_recv, sibling).wait_recv()
    out_ref[...] = acc[1, col] + jnp.sum(back2[...].astype(jnp.float32), axis=0) + b2_ref[...]

    for i in range(len(FAR_Y)):
        r1_copy(i).wait_send()
        r2_copy(i).wait_send()

    @pl.when(core == 0)
    def _():
        half_copy().wait_send()
        r1_own().wait_send()

    @pl.when(core == 1)
    def _():
        for layer in range(2):
            for i in range(len(FAR_Z)):
                z_copy(layer, i).wait_send()

            @pl.loop(0, NZ)
            def _(dz):
                for i in range(len(FAR_X)):
                    x_copy(layer, dz, i).wait_send()
                c_copy(layer, dz, 0, 1, 0).wait_send()
                c_copy(layer, dz, 1, NX - 1, 1).wait_send()


def on_device(
    features, tile_coords, tile_count, tile_values, w_first, bias_first, w_second, bias_second
):
    coords = tile_coords[0, 0]
    slots = jnp.arange(SLOTS, dtype=jnp.int32)
    place = jnp.where(slots < tile_count[0, 0], coords[:, 0] * (NX * NZ) + coords[:, 1], -1)
    hit = place[:, None] == jnp.arange(RT * NX * NZ, dtype=jnp.int32)[None, :]
    slot_of = jnp.min(jnp.where(hit, slots[:, None], SLOTS), axis=0)
    vmem = pl.BlockSpec(memory_space=pltpu.VMEM)
    dma = pltpu.SemaphoreType.DMA
    return pl.pallas_call(
        kernel,
        out_shape=jax.ShapeDtypeStruct((64, TILE), jnp.float32),
        in_specs=[
            pl.BlockSpec(memory_space=pltpu.SMEM), vmem, pl.BlockSpec(memory_space=pl.ANY), vmem, vmem, vmem, vmem,
        ],
        out_specs=vmem,
        scratch_shapes=[
            pltpu.VMEM((SLOTS + 1, TILE, TILE), jnp.bfloat16),
            pltpu.VMEM((64, TILE), jnp.bfloat16),
            pltpu.VMEM((2, NZ, NX, TILE, TILE), jnp.bfloat16),
            pltpu.VMEM((2, NY, 64, TILE), jnp.float32),
            pltpu.VMEM((2, NY, 64, TILE), jnp.float32),
            pltpu.VMEM((NY, 64, TILE), jnp.bfloat16),
            pltpu.VMEM((NY - 1, 64, TILE), jnp.bfloat16),
            dma, dma, dma,
            dma((2, 11)), dma((2, NZ)), dma((2, NZ, 3)), dma((2, NZ)), dma((2, NZ, 2)), dma((2, NZ)),
            dma((8,)), dma((2,)), dma((7,)), dma,
        ],
        compiler_params=pltpu.CompilerParams(
            collective_id=0, has_side_effects=True, vmem_limit_bytes=32 * 2**20
        ),
        cost_estimate=pl.CostEstimate(flops=3 * 10**9, bytes_accessed=2 * 10**6, transcendentals=0),
    )(
        slot_of, features, tile_values[0, 0], w_first, bias_first.reshape(1, TILE), w_second, bias_second.reshape(1, TILE)
    )


def solution(mesh):
    return jax.shard_map(
        on_device,
        mesh=mesh,
        in_specs=(
            P(("row", "col"), None),
            P("row", "col", None, None),
            P("row", "col"),
            P("row", "col", None, None, None),
            P(),
            P(),
            P(),
            P(),
        ),
        out_specs=P(("row", "col"), None),
        check_vma=False,
    )
```

```python
import jax
import jax.numpy as jnp
from jax import lax
from jax.experimental import pallas as pl
from jax.experimental.pallas import tpu as pltpu
from jax.sharding import PartitionSpec as P

MESH = pl.DeviceIdType.MESH
NX, NZ, NY = 4, 12, 8
TILE, RT, SLOTS, NODE = 128, 4, 54, 64
SEND_Z = (2, -2, 6, 5, -5, 4, -4, 3, -3, 1, -1)
FAR_X = (2, 1, -1)
FAR_Y = (4, 3, -3, 2, -2, 1, -1)
NEAR_Z = (1, NZ - 1)
BY_Z = (2, 10, 3, 9, 4, 8, 5, 7, 6)
GROUPS = (0, 2, 10, 3, 9, 1, 11, 4, 8, 5, 7, 6)
LAG = 3
WIDE_Y, NARROW_Y = (2, -2, 1, -1), (4, 3, -3)


def kernel(
    count_ref, coords_hbm, feat_hbm, tiles_hbm, w1_hbm, b1_hbm, w2_hbm, b2_hbm, out_ref,
    coords, feat, tiles, w1, b1, w2, b2, table_v, table, zb, acc, wide, narrow, part2, back2,
    load_sem, table_sem, z_send, z_recv, zx_send, x_send, x_recv, c_send, c_recv,
    r1_send, r1_recv, r2_send, r2_recv,
):
    row, col = lax.axis_index("row"), lax.axis_index("col")
    core = row % 2
    chip = row // 2
    z, x = chip % NZ, chip // NZ

    def at(dx, dz, c, dy=0):
        return (
            (((x + dx + NX) % NX) * NZ + (z + dz + NZ) % NZ) * 2 + c,
            (col + dy + NY) % NY,
        )

    def remote(src, dst, send, recv, to):
        return pltpu.make_async_remote_copy(
            src_ref=src, dst_ref=dst, send_sem=send, recv_sem=recv, device_id=to, device_id_type=MESH
        )

    sibling = at(0, 0, 1 - core)

    loads = [
        pltpu.make_async_copy(src, dst, load_sem.at[i])
        for i, (src, dst) in enumerate(
            (
                (feat_hbm, feat), (w1_hbm, w1), (coords_hbm, coords),
                (tiles_hbm, tiles.at[pl.ds(0, SLOTS)]), (b1_hbm, b1), (w2_hbm, w2), (b2_hbm, b2),
            )
        )
    ]
    for load in loads:
        load.start()

    barrier = pltpu.get_barrier_semaphore()
    peers = [at(0, d, core) for d in SEND_Z] + [at(0, 0, core, d) for d in FAR_Y]
    peers += [at(d, 0, core) for d in FAR_X] + [sibling]
    for to in peers:
        pl.semaphore_signal(barrier, inc=1, device_id=to, device_id_type=MESH)

    loads[0].wait()
    loads[1].wait()
    zb[0, 0, 0, core] = jnp.dot(
        feat[...], w1[...], precision=lax.Precision.HIGHEST, preferred_element_type=jnp.float32
    ).astype(jnp.bfloat16)

    pl.semaphore_wait(barrier, len(peers))

    def z_copy(layer, i):
        d = SEND_Z[i]
        return remote(
            zb.at[layer, 0, 0, core], zb.at[layer, -d % NZ, 0, core],
            z_send.at[layer, i], z_recv.at[layer, -d % NZ], at(0, d, core),
        )

    def x_copy(layer, dz, i):
        d = FAR_X[i]
        return remote(
            zb.at[layer, dz, 0, core], zb.at[layer, dz, -d % NX, core],
            x_send.at[layer, dz, i], x_recv.at[layer, dz], at(d, 0, core),
        )

    def c_copy(layer, dz, i):
        block = zb.at[layer, dz, pl.ds(1, NX - 1) if i else 0, core]
        return remote(block, block, c_send.at[layer, dz, i], c_recv.at[layer, dz], sibling)

    def multiply(layer, dz):
        za = (z + dz) % NZ
        places = [((x + dx) % NX) * NZ + za for dx in range(NX)]
        rhs = zb[layer, dz].reshape(NX * TILE, TILE)
        for r in range(RT):
            lhs = jnp.concatenate(
                [tiles[table[0, r * NX * NZ + p]] for p in places], axis=1
            )
            acc[layer, 2 * r : 2 * r + 2] += jnp.dot(
                lhs, rhs, preferred_element_type=jnp.float32
            ).reshape(2, NODE, TILE)

    def pass_x_on(layer, i):
        d = (1, -1)[i]
        return remote(
            zb.at[layer, 0, pl.ds(1, NX - 1), core], zb.at[layer, -d % NZ, pl.ds(1, NX - 1), core],
            zx_send.at[layer, i], x_recv.at[layer, -d % NZ], at(0, d, core),
        )

    def arrived(block, recv):
        remote(block, block, z_send.at[0, 0], recv, sibling).wait_recv()

    def start_gather(layer):
        for i in range(len(FAR_X)):
            x_copy(layer, 0, i).start()
        for i in range(len(SEND_Z)):
            z_copy(layer, i).start()
        c_copy(layer, 0, 0).start()
        acc[layer] = jnp.zeros((NY, NODE, TILE), jnp.float32)

    def take_z(layer, dz):
        arrived(zb.at[layer, dz, 0, core], z_recv.at[layer, dz])
        if dz not in NEAR_Z:
            for i in range(len(FAR_X)):
                x_copy(layer, dz, i).start()
        c_copy(layer, dz, 0).start()

    def take_x(layer, dz):
        arrived(zb.at[layer, dz, pl.ds(1, NX - 1), core], x_recv.at[layer, dz])
        if dz == 0:
            for i in range(2):
                pass_x_on(layer, i).start()
        c_copy(layer, dz, 1).start()

    def use(layer, dz):
        arrived(zb.at[layer, dz, :, 1 - core], c_recv.at[layer, dz])
        multiply(layer, dz)

    def gather_multiply(layer):
        take_z(layer, BY_Z[0])
        take_z(layer, BY_Z[1])
        take_x(layer, 0)
        for dz in BY_Z[2:] + NEAR_Z:
            take_z(layer, dz)
        for t in range(1, NZ + LAG):
            if t < NZ:
                take_x(layer, GROUPS[t])
            if t >= LAG:
                use(layer, GROUPS[t - LAG])

    def drain(layer):
        for i in range(len(SEND_Z)):
            z_copy(layer, i).wait_send()
        for i in range(2):
            pass_x_on(layer, i).wait_send()
        for dz in range(NZ):
            for i in range(len(FAR_X) if dz not in NEAR_Z else 0):
                x_copy(layer, dz, i).wait_send()
            for i in range(2):
                c_copy(layer, dz, i).wait_send()

    start_gather(0)
    loads[2].wait()
    lane = lax.broadcasted_iota(jnp.int32, (SLOTS, SLOTS), 1)
    slot = lax.broadcasted_iota(jnp.int32, (SLOTS, SLOTS), 0)
    place = coords[0:1, :] * (NX * NZ) + coords[1:2, :]
    place = jnp.where(lane[0:1] < count_ref[0, 0], place, -1)
    place = jnp.max(jnp.where(lane == slot, place, -1), axis=1, keepdims=True)
    hit = place == lax.broadcasted_iota(jnp.int32, (SLOTS, 2 * TILE), 1)
    used = jnp.where(hit, lax.broadcasted_iota(jnp.int32, (SLOTS, 2 * TILE), 0), SLOTS)
    table_v[...] = jnp.min(used, axis=0, keepdims=True)
    to_table = pltpu.make_async_copy(table_v, table, table_sem)
    to_table.start()
    tiles[SLOTS] = jnp.zeros((TILE, TILE), jnp.bfloat16)
    for load in loads[3:]:
        load.wait()
    to_table.wait()
    gather_multiply(0)

    def wide_copy(i):
        d = WIDE_Y[i]
        return remote(
            acc.at[0, (col + d + NY) % NY], wide.at[WIDE_Y.index(-d)], r1_send.at[i], r1_recv.at[0], at(0, 0, core, d)
        )

    def narrow_copy(i):
        d = NARROW_Y[i]
        slot = (0, 2, 1)[i]
        return remote(narrow.at[0, i], narrow.at[1, slot], r1_send.at[4 + i], r1_recv.at[1], at(0, 0, core, d))

    for i, d in enumerate(NARROW_Y):
        narrow[0, i] = acc[0, (col + d + NY) % NY].astype(jnp.bfloat16)
        narrow_copy(i).start()
    for i in range(len(WIDE_Y)):
        wide_copy(i).start()
    total = acc[0, col] + b1[...]
    arrived(wide, r1_recv.at[0])
    total += jnp.sum(wide[...], axis=0)
    arrived(narrow.at[1], r1_recv.at[1])
    total += jnp.sum(narrow[1].astype(jnp.float32), axis=0)
    hidden = jnp.maximum(total, 0.0)
    zb[1, 0, 0, core] = jnp.dot(
        hidden, w2[...], precision=lax.Precision.HIGHEST, preferred_element_type=jnp.float32
    ).astype(jnp.bfloat16)

    start_gather(1)
    gather_multiply(1)
    part2[...] = acc[1].astype(jnp.bfloat16)

    def r2_copy(i):
        d = FAR_Y[i]
        return remote(
            part2.at[(col + d + NY) % NY], back2.at[-d % NY - 1], r2_send.at[i], r2_recv, at(0, 0, core, d)
        )

    for i in range(len(FAR_Y)):
        r2_copy(i).start()

    for i in range(len(WIDE_Y)):
        wide_copy(i).wait_send()
    for i in range(len(NARROW_Y)):
        narrow_copy(i).wait_send()
    drain(0)
    drain(1)

    own = acc[1, col] + b2[...]
    arrived(back2, r2_recv)
    out_ref[...] = own + jnp.sum(back2[...].astype(jnp.float32), axis=0)
    for i in range(len(FAR_Y)):
        r2_copy(i).wait_send()


def on_device(
    features, tile_coords, tile_count, tile_values, w_first, bias_first, w_second, bias_second
):
    hbm = pl.BlockSpec(memory_space=pltpu.HBM)
    dma = pltpu.SemaphoreType.DMA
    bf16, f32, i32 = jnp.bfloat16, jnp.float32, jnp.int32
    in_hbm = (
        tile_coords[0, 0].T, features, tile_values[0, 0],
        w_first, bias_first.reshape(1, TILE), w_second, bias_second.reshape(1, TILE),
    )
    return pl.pallas_call(
        kernel,
        out_shape=jax.ShapeDtypeStruct((NODE, TILE), f32),
        in_specs=[pl.BlockSpec(memory_space=pltpu.SMEM)] + [hbm] * 7,
        out_specs=pl.BlockSpec(memory_space=pltpu.VMEM),
        scratch_shapes=[
            pltpu.VMEM((2, SLOTS), i32),
            pltpu.VMEM((NODE, TILE), f32),
            pltpu.VMEM((SLOTS + 1, TILE, TILE), bf16),
            pltpu.VMEM((TILE, TILE), f32),
            pltpu.VMEM((1, TILE), f32),
            pltpu.VMEM((TILE, TILE), f32),
            pltpu.VMEM((1, TILE), f32),
            pltpu.VMEM((1, 2 * TILE), i32),
            pltpu.SMEM((1, 2 * TILE), i32),
            pltpu.VMEM((2, NZ, NX, 2, NODE, TILE), bf16),
            pltpu.VMEM((2, NY, NODE, TILE), f32),
            pltpu.VMEM((4, NODE, TILE), f32),
            pltpu.VMEM((2, 3, NODE, TILE), bf16),
            pltpu.VMEM((NY, NODE, TILE), bf16),
            pltpu.VMEM((NY - 1, NODE, TILE), bf16),
            dma((7,)), dma,
            dma((2, 11)), dma((2, NZ)), dma((2, 2)), dma((2, NZ, 3)), dma((2, NZ)), dma((2, NZ, 2)), dma((2, NZ)),
            dma((7,)), dma((2,)), dma((7,)), dma,
        ],
        compiler_params=pltpu.CompilerParams(
            collective_id=0, has_side_effects=True, vmem_limit_bytes=48 * 2**20
        ),
        cost_estimate=pl.CostEstimate(flops=3 * 10**9, bytes_accessed=2 * 10**6, transcendentals=0),
    )(tile_count, *[pltpu.with_memory_space_constraint(a, pltpu.HBM) for a in in_hbm])


def solution(mesh):
    return jax.shard_map(
        on_device,
        mesh=mesh,
        in_specs=(
            P(("row", "col"), None),
            P("row", "col", None, None),
            P("row", "col"),
            P("row", "col", None, None, None),
            P(),
            P(),
            P(),
            P(),
        ),
        out_specs=P(("row", "col"), None),
        check_vma=False,
    )
```

```python
import jax
import jax.numpy as jnp
from jax import lax
from jax.experimental import pallas as pl
from jax.experimental.pallas import tpu as pltpu
from jax.sharding import PartitionSpec as P

MESH = pl.DeviceIdType.MESH
NX, NZ, NY = 4, 12, 8
TILE, RT, SLOTS, NODE = 128, 4, 54, 64
SEND_Z = (2, -2, 3, -3, 4, -4, 5, -5, 6, 1, -1)
TAKE_Z = (2, -2, 3, -3, 4, -4, 5, -5, 6, 1, -1)
NEAR_Z = (1, -1)
EARLY = (0, 2, -2)
GROUPS = (0, 2, -2, 3, -3, 1, -1, 4, -4, 5, -5, 6)
RANK = {d: k for k, d in enumerate(GROUPS)} | {-6: GROUPS.index(6)}
LAG = 3
WIDE_Y, NARROW_Y = (1, -1), (4, 3, -3, 2, -2)
FAR_Y = (4, 3, -3, 2, -2, 1, -1)


def kernel(
    count_ref, coords_hbm, feat_hbm, tiles_hbm, w1_hbm, b1_hbm, w2_hbm, b2_hbm, out_ref,
    coords, feat, tiles, w1, b1, w2, b2, table_v, table, half, zb, acc, wide, narrow, narrow_out, own0, part2, back2,
    load_sem, table_sem, half_send, half_recv, z_send, z_recv, zx_send, x_send, x_recv, c_send, c_recv,
    r1_send, r1_recv, own_send, own_recv, r2_send, r2_recv,
):
    row, col = lax.axis_index("row"), lax.axis_index("col")
    core = row % 2
    chip = row // 2
    z, x = chip % NZ, chip // NZ

    def at(dx, dz, c, dy=0):
        return (
            (((x + dx + NX) % NX) * NZ + (z + dz + NZ) % NZ) * 2 + c,
            (col + dy + NY) % NY,
        )

    def remote(src, dst, send, recv, to):
        return pltpu.make_async_remote_copy(
            src_ref=src, dst_ref=dst, send_sem=send, recv_sem=recv, device_id=to, device_id_type=MESH
        )

    def arrived(block, recv):
        remote(block, block, z_send.at[0, 0], recv, sibling).wait_recv()

    loads = [
        pltpu.make_async_copy(src, dst, load_sem.at[i])
        for i, (src, dst) in enumerate(
            (
                (feat_hbm, feat), (w1_hbm, w1), (coords_hbm, coords),
                (tiles_hbm, tiles.at[pl.ds(0, SLOTS)]), (b1_hbm, b1), (w2_hbm, w2), (b2_hbm, b2),
            )
        )
    ]
    for load in loads[:2]:
        load.start()

    sibling = at(0, 0, 1 - core)
    barrier = pltpu.get_barrier_semaphore()

    def signal(to):
        pl.semaphore_signal(barrier, inc=1, device_id=to, device_id_type=MESH)

    @pl.when(core == 0)
    def _():
        for d in (6, 5, -5, 4, -4, 3, -3, 2, -2, 1, -1):
            signal(at(0, d, 1))

    @pl.when(core == 1)
    def _():
        for d in FAR_Y:
            signal(at(0, 0, 1, d))
        for d in (2, 1, -1):
            signal(at(d, 0, 0))
        signal(at(2, 0, 1))
        for d in NEAR_Z:
            signal(at(0, d, 1))

    signal(sibling)
    for d in FAR_Y:
        signal(at(0, 0, 0, d))

    for load in loads[2:]:
        load.start()
    loads[0].wait()
    loads[1].wait()
    mixed = jnp.dot(
        feat[...], w1[...], precision=lax.Precision.HIGHEST, preferred_element_type=jnp.float32
    ).astype(jnp.bfloat16)

    def half_copy():
        return remote(half, zb.at[0, 0, 0, pl.ds(0, NODE)], half_send, half_recv, sibling)

    def z_copy(layer, i):
        d = SEND_Z[i]
        return remote(
            zb.at[layer, 0, 0], zb.at[layer, RANK[-d], 0],
            z_send.at[layer, i], z_recv.at[layer, RANK[-d]], at(0, d, 0),
        )

    def x_copy(layer, dz, d):
        k, i = RANK[dz], d % NX - 1
        return remote(
            zb.at[layer, k, 0], zb.at[layer, k, -d % NX],
            x_send.at[layer, k, i], x_recv.at[layer, k], at(d, 0, 1),
        )

    def pass_x_on(layer, i):
        d = NEAR_Z[i]
        return remote(
            zb.at[layer, 0, pl.ds(1, NX - 1)], zb.at[layer, RANK[-d], pl.ds(1, NX - 1)],
            zx_send.at[layer, i], x_recv.at[layer, RANK[-d]], at(0, d, 1),
        )

    def c_one(layer, dz):
        block = zb.at[layer, RANK[dz], 0]
        return remote(block, block, c_send.at[layer, RANK[dz], 0], c_recv.at[layer, RANK[dz], 0], sibling)

    def c_rest(layer, dz):
        block = zb.at[layer, RANK[dz], pl.ds(1, NX - 1)]
        return remote(block, block, c_send.at[layer, RANK[dz], 1], c_recv.at[layer, RANK[dz], 1], sibling)

    def multiply(layer, dz):
        za = (z + dz + NZ) % NZ
        places = [((x + dx) % NX) * NZ + za for dx in range(NX)]
        rhs = zb[layer, RANK[dz]].reshape(NX * TILE, TILE)
        for r in range(RT):
            lhs = jnp.concatenate(
                [tiles[table[0, r * NX * NZ + p]] for p in places], axis=1
            )
            acc[layer, 2 * r : 2 * r + 2] += jnp.dot(
                lhs, rhs, preferred_element_type=jnp.float32
            ).reshape(2, NODE, TILE)

    def start_gather(layer):
        c_one(layer, 0).start()
        for i in range(len(SEND_Z)):
            z_copy(layer, i).start()

    def sends_of_x(dz):
        return (2, 1, -1) if dz in EARLY else (1, -1)

    def gather_0(layer):
        arrived(zb.at[layer, 0, 0], c_recv.at[layer, 0, 0])
        for d in sends_of_x(0):
            x_copy(layer, 0, d).start()
        for dz in TAKE_Z:
            arrived(zb.at[layer, RANK[dz], 0], z_recv.at[layer, RANK[dz]])
            if dz not in NEAR_Z:
                for d in sends_of_x(dz):
                    x_copy(layer, dz, d).start()
            c_one(layer, dz).start()
        for dz in GROUPS:
            arrived(zb.at[layer, RANK[dz], pl.ds(1, NX - 1)], c_recv.at[layer, RANK[dz], 1])
            multiply(layer, dz)

    def take_c(layer, dz):
        arrived(zb.at[layer, RANK[dz], 0], c_recv.at[layer, RANK[dz], 0])
        if dz not in NEAR_Z + EARLY:
            x_copy(layer, dz, 2).start()

    def take_x(layer, dz):
        arrived(zb.at[layer, RANK[dz], pl.ds(1, NX - 1)], x_recv.at[layer, RANK[dz]])
        if dz == 0:
            for i in range(2):
                pass_x_on(layer, i).start()
        c_rest(layer, dz).start()

    def gather_1(layer):
        for dz in (2, -2, 3, -3):
            take_c(layer, dz)
        take_x(layer, 0)
        for dz in TAKE_Z[4:]:
            take_c(layer, dz)
        for t in range(1, NZ + LAG):
            if t < NZ:
                take_x(layer, GROUPS[t])
            if t >= LAG:
                multiply(layer, GROUPS[t - LAG])

    def drain_0(layer):
        for dz in GROUPS:
            if dz not in NEAR_Z:
                for d in sends_of_x(dz):
                    x_copy(layer, dz, d).wait_send()
            if dz != 0:
                c_one(layer, dz).wait_send()

    def drain_1(layer):
        c_one(layer, 0).wait_send()
        for i in range(len(SEND_Z)):
            z_copy(layer, i).wait_send()
        for i in range(2):
            pass_x_on(layer, i).wait_send()
        for dz in GROUPS:
            if dz not in NEAR_Z + EARLY:
                x_copy(layer, dz, 2).wait_send()
            c_rest(layer, dz).wait_send()

    @pl.when(core == 0)
    def _():
        half[...] = mixed
        pl.semaphore_wait(barrier, 3 + 1 + 7 + 7)
        half_copy().start()

    @pl.when(core == 1)
    def _():
        zb[0, 0, 0, NODE:TILE] = mixed
        pl.semaphore_wait(barrier, 11 + 2 + 1 + 1 + 7)
        half_copy().wait_recv()
        start_gather(0)

    loads[2].wait()
    lane = lax.broadcasted_iota(jnp.int32, (SLOTS, SLOTS), 1)
    slot = lax.broadcasted_iota(jnp.int32, (SLOTS, SLOTS), 0)
    place = coords[0:1, :] * (NX * NZ) + coords[1:2, :]
    place = jnp.where(lane[0:1] < count_ref[0, 0], place, -1)
    place = jnp.max(jnp.where(lane == slot, place, -1), axis=1, keepdims=True)
    hit = place == lax.broadcasted_iota(jnp.int32, (SLOTS, 2 * TILE), 1)
    used = jnp.where(hit, lax.broadcasted_iota(jnp.int32, (SLOTS, 2 * TILE), 0), SLOTS)
    table_v[...] = jnp.min(used, axis=0, keepdims=True)
    to_table = pltpu.make_async_copy(table_v, table, table_sem)
    to_table.start()
    tiles[SLOTS] = jnp.zeros((TILE, TILE), jnp.bfloat16)
    acc[...] = jnp.zeros((2, NY, NODE, TILE), jnp.float32)
    for load in loads[3:]:
        load.wait()
    to_table.wait()

    def wide_copy(i):
        d = WIDE_Y[i]
        return remote(
            acc.at[0, (col + d + NY) % NY], wide.at[core, WIDE_Y.index(-d)],
            r1_send.at[i], r1_recv.at[core, 0], at(0, 0, 1, d),
        )

    def narrow_copy(i):
        d = NARROW_Y[i]
        return remote(
            narrow_out.at[i], narrow.at[core, NARROW_Y.index(d if d == 4 else -d)],
            r1_send.at[len(WIDE_Y) + i], r1_recv.at[core, 1], at(0, 0, 1, d),
        )

    def own_copy():
        return remote(acc.at[0, col], own0, own_send, own_recv, sibling)

    def send_partials():
        for i, d in enumerate(NARROW_Y):
            narrow_out[i] = acc[0, (col + d + NY) % NY].astype(jnp.bfloat16)
            narrow_copy(i).start()
        for i in range(len(WIDE_Y)):
            wide_copy(i).start()

    @pl.when(core == 0)
    def _():
        gather_0(0)
        send_partials()
        own_copy().start()
        gather_0(1)

    @pl.when(core == 1)
    def _():
        gather_1(0)
        send_partials()
        own = acc[0, col] + b1[...]
        arrived(own0, own_recv)
        totals = [own0[...] + b1[...], own]
        for c in (1, 0):
            arrived(wide.at[c], r1_recv.at[c, 0])
            totals[c] += jnp.sum(wide[c], axis=0)
            arrived(narrow.at[c], r1_recv.at[c, 1])
            totals[c] += jnp.sum(narrow[c].astype(jnp.float32), axis=0)
        hidden = jnp.maximum(jnp.concatenate(totals, axis=0), 0.0)
        zb[1, 0, 0] = jnp.dot(
            hidden, w2[...], precision=lax.Precision.HIGHEST, preferred_element_type=jnp.float32
        ).astype(jnp.bfloat16)
        start_gather(1)
        gather_1(1)

    part2[...] = acc[1].astype(jnp.bfloat16)

    def r2_copy(i):
        d = FAR_Y[i]
        return remote(
            part2.at[(col + d + NY) % NY], back2.at[-d % NY - 1], r2_send.at[i], r2_recv, at(0, 0, core, d)
        )

    for i in range(len(FAR_Y)):
        r2_copy(i).start()

    for i in range(len(WIDE_Y)):
        wide_copy(i).wait_send()
    for i in range(len(NARROW_Y)):
        narrow_copy(i).wait_send()

    @pl.when(core == 0)
    def _():
        half_copy().wait_send()
        own_copy().wait_send()
        drain_0(0)
        drain_0(1)

    @pl.when(core == 1)
    def _():
        drain_1(0)
        drain_1(1)

    own = acc[1, col] + b2[...]
    arrived(back2, r2_recv)
    out_ref[...] = own + jnp.sum(back2[...].astype(jnp.float32), axis=0)
    for i in range(len(FAR_Y)):
        r2_copy(i).wait_send()


def on_device(
    features, tile_coords, tile_count, tile_values, w_first, bias_first, w_second, bias_second
):
    hbm = pl.BlockSpec(memory_space=pltpu.HBM)
    dma = pltpu.SemaphoreType.DMA
    bf16, f32, i32 = jnp.bfloat16, jnp.float32, jnp.int32
    in_hbm = (
        tile_coords[0, 0].T, features, tile_values[0, 0],
        w_first, bias_first.reshape(1, TILE), w_second, bias_second.reshape(1, TILE),
    )
    return pl.pallas_call(
        kernel,
        out_shape=jax.ShapeDtypeStruct((NODE, TILE), f32),
        in_specs=[pl.BlockSpec(memory_space=pltpu.SMEM)] + [hbm] * 7,
        out_specs=pl.BlockSpec(memory_space=pltpu.VMEM),
        scratch_shapes=[
            pltpu.VMEM((2, SLOTS), i32),
            pltpu.VMEM((NODE, TILE), f32),
            pltpu.VMEM((SLOTS + 1, TILE, TILE), bf16),
            pltpu.VMEM((TILE, TILE), f32),
            pltpu.VMEM((1, TILE), f32),
            pltpu.VMEM((TILE, TILE), f32),
            pltpu.VMEM((1, TILE), f32),
            pltpu.VMEM((1, 2 * TILE), i32),
            pltpu.SMEM((1, 2 * TILE), i32),
            pltpu.VMEM((NODE, TILE), bf16),
            pltpu.VMEM((2, NZ, NX, TILE, TILE), bf16),
            pltpu.VMEM((2, NY, NODE, TILE), f32),
            pltpu.VMEM((2, 2, NODE, TILE), f32),
            pltpu.VMEM((2, 5, NODE, TILE), bf16),
            pltpu.VMEM((5, NODE, TILE), bf16),
            pltpu.VMEM((NODE, TILE), f32),
            pltpu.VMEM((NY, NODE, TILE), bf16),
            pltpu.VMEM((NY - 1, NODE, TILE), bf16),
            dma((7,)), dma, dma, dma,
            dma((2, 11)), dma((2, NZ)), dma((2, 2)), dma((2, NZ, 3)), dma((2, NZ)), dma((2, NZ, 2)), dma((2, NZ, 2)),
            dma((7,)), dma((2, 2)), dma, dma, dma((7,)), dma,
        ],
        compiler_params=pltpu.CompilerParams(
            collective_id=0, has_side_effects=True, vmem_limit_bytes=48 * 2**20
        ),
        cost_estimate=pl.CostEstimate(flops=3 * 10**9, bytes_accessed=2 * 10**6, transcendentals=0),
    )(tile_count, *[pltpu.with_memory_space_constraint(a, pltpu.HBM) for a in in_hbm])


def solution(mesh):
    return jax.shard_map(
        on_device,
        mesh=mesh,
        in_specs=(
            P(("row", "col"), None),
            P("row", "col", None, None),
            P("row", "col"),
            P("row", "col", None, None, None),
            P(),
            P(),
            P(),
            P(),
        ),
        out_specs=P(("row", "col"), None),
        check_vma=False,
    )
```

```python
import functools

import jax
import jax.numpy as jnp
from jax import lax
from jax.experimental import pallas as pl
from jax.experimental.pallas import tpu as pltpu
from jax.sharding import PartitionSpec as P

MESH = pl.DeviceIdType.MESH
NX, NZ, NY = 4, 12, 8
TILE, RT, SLOTS, NODE = 128, 4, 54, 64
OPT = dict(
    nl=2,
    SEND_Z=(2, -2, 3, -3, 4, -4, 5, -5, 6, 1, -1),
    BY_Z=(2, -2, 3, -3, 4, -4, 5, -5, 6),
    ZCOUNT=4,
    BUNDLES=((0,), (2,), (-2,), (3,), (-3,), (4,), (-4,), (1,), (-1,), (5,), (-5,), (6,)),
    LAG=6,
    X=(2, 1, -1),
    WIDE_Y=(), NARROW_Y=(4, 3, -3, 2, -2, 1, -1),
)


def kernel(
    opt,
    count_ref, coords_hbm, feat_hbm, tiles_hbm, w1_hbm, b1_hbm, w2_hbm, b2_hbm, out_ref,
    coords, feat, tiles, w1, b1, w2, b2, table_v, table, zb, acc, wide, narrow, part2, back2,
    load_sem, table_sem, z_send, z_recv, zx_send, x_send, x_recv, c_send, c_recv,
    r1_send, r1_recv, r2_send, r2_recv,
):
    nl, SEND_Z, BY_Z, BUNDLES, LAG, FAR_X = opt["nl"], opt["SEND_Z"], opt["BY_Z"], opt["BUNDLES"], opt["LAG"], opt["X"]
    WIDE_Y, NARROW_Y = opt["WIDE_Y"], opt["NARROW_Y"]
    NEAR_Z = (1, -1)
    order = [d for b in BUNDLES for d in b]
    rank = {d: k for k, d in enumerate(order)}
    rank[-6] = rank[6]
    row, col = lax.axis_index("row"), lax.axis_index("col")
    core = row % 2
    chip = row // 2
    z, x = chip % NZ, chip // NZ

    def at(dx, dz, c, dy=0):
        return (
            (((x + dx + NX) % NX) * NZ + (z + dz + NZ) % NZ) * 2 + c,
            (col + dy + NY) % NY,
        )

    def remote(src, dst, send, recv, to):
        return pltpu.make_async_remote_copy(
            src_ref=src, dst_ref=dst, send_sem=send, recv_sem=recv, device_id=to, device_id_type=MESH
        )

    sibling = at(0, 0, 1 - core)

    barrier = pltpu.get_barrier_semaphore()
    peers = [at(0, d, core) for d in (6, 5, -5, 4, -4)] + [at(0, 0, core, d) for d in (4, 3, -3)]
    peers += [at(0, d, core) for d in (3, -3, 2, -2, 1, -1)] + [at(0, 0, core, d) for d in (2, -2, 1, -1)]
    peers += [at(d, 0, core) for d in FAR_X] + [sibling]
    for to in peers:
        pl.semaphore_signal(barrier, inc=1, device_id=to, device_id_type=MESH)

    loads = [
        pltpu.make_async_copy(src, dst, load_sem.at[i])
        for i, (src, dst) in enumerate(
            (
                (feat_hbm, feat), (w1_hbm, w1), (coords_hbm, coords),
                (tiles_hbm, tiles.at[pl.ds(0, SLOTS)]), (b1_hbm, b1), (w2_hbm, w2), (b2_hbm, b2),
            )
        )
    ]
    for load in loads:
        load.start()

    loads[0].wait()
    loads[1].wait()
    zb[0, core, 0, 0] = jnp.dot(
        feat[...], w1[...], precision=lax.Precision.HIGHEST, preferred_element_type=jnp.float32
    ).astype(jnp.bfloat16)

    pl.semaphore_wait(barrier, len(peers))

    def z_copy(layer, i):
        d = SEND_Z[i]
        return remote(
            zb.at[layer, core, 0, 0], zb.at[layer, core, rank[-d], 0],
            z_send.at[layer, i], z_recv.at[layer, rank[-d]], at(0, d, core),
        )

    def x_copy(layer, dz, i):
        d, k = FAR_X[i], rank[dz]
        return remote(
            zb.at[layer, core, k, 0], zb.at[layer, core, k, -d % NX],
            x_send.at[layer, k, i], x_recv.at[layer, k], at(d, 0, core),
        )

    def pass_x_on(layer, i):
        d = NEAR_Z[i]
        return remote(
            zb.at[layer, core, 0, pl.ds(1, NX - 1)], zb.at[layer, core, rank[-d], pl.ds(1, NX - 1)],
            zx_send.at[layer, i], x_recv.at[layer, rank[-d]], at(0, d, core),
        )

    def c_copy(layer, b):
        first, size = rank[BUNDLES[b][0]], len(BUNDLES[b])
        block = zb.at[layer, core, pl.ds(first, size)]
        return remote(block, block, c_send.at[layer, b], c_recv.at[layer, b], sibling)

    def arrived(block, recv):
        remote(block, block, z_send.at[0, 0], recv, sibling).wait_recv()

    def multiply(layer, dz):
        za = (z + dz + NZ) % NZ
        places = [((x + dx) % NX) * NZ + za for dx in range(NX)]
        k = rank[dz]
        rhs = jnp.concatenate([zb[layer, c, k, dx] for dx in range(NX) for c in range(2)], axis=0)
        for r in range(RT):
            lhs = jnp.concatenate(
                [tiles[table[0, r * NX * NZ + p]] for p in places], axis=1
            )
            acc[layer, 2 * r : 2 * r + 2] += jnp.dot(
                lhs, rhs, preferred_element_type=jnp.float32
            ).reshape(2, NODE, TILE)

    def start_gather(layer):
        for i in range(len(FAR_X)):
            x_copy(layer, 0, i).start()
        for i in range(len(SEND_Z)):
            z_copy(layer, i).start()
        acc[layer] = jnp.zeros((NY, NODE, TILE), jnp.float32)

    def take_z(layer, dz):
        k = rank[dz]
        arrived(zb.at[layer, core, k, 0], z_recv.at[layer, k])
        if dz not in NEAR_Z:
            for i in range(len(FAR_X)):
                x_copy(layer, dz, i).start()

    def take_x(layer, dz):
        arrived(zb.at[layer, core, rank[dz], pl.ds(1, NX - 1)], x_recv.at[layer, rank[dz]])
        if dz == 0:
            for i in range(2):
                pass_x_on(layer, i).start()

    def gather_multiply(layer):
        for dz in BY_Z[: opt["ZCOUNT"]]:
            take_z(layer, dz)
        take_x(layer, 0)
        for dz in BY_Z[opt["ZCOUNT"] :] + NEAR_Z:
            take_z(layer, dz)
        for t in range(len(BUNDLES) + LAG):
            if t < len(BUNDLES):
                for dz in BUNDLES[t]:
                    if dz != 0:
                        take_x(layer, dz)
                c_copy(layer, t).start()
            if t >= LAG:
                b = t - LAG
                first, size = rank[BUNDLES[b][0]], len(BUNDLES[b])
                arrived(zb.at[layer, 1 - core, pl.ds(first, size)], c_recv.at[layer, b])
                for dz in BUNDLES[b]:
                    multiply(layer, dz)

    def drain(layer):
        for i in range(len(SEND_Z)):
            z_copy(layer, i).wait_send()
        for i in range(2):
            pass_x_on(layer, i).wait_send()
        for dz in order:
            for i in range(len(FAR_X) if dz not in NEAR_Z else 0):
                x_copy(layer, dz, i).wait_send()
        for b in range(len(BUNDLES)):
            c_copy(layer, b).wait_send()

    def wide_copy(layer, i):
        d = WIDE_Y[i]
        return remote(
            acc.at[layer, (col + d + NY) % NY], wide.at[layer, WIDE_Y.index(-d)],
            r1_send.at[layer, i], r1_recv.at[layer, 0], at(0, 0, core, d),
        )

    def narrow_copy(layer, i):
        d = NARROW_Y[i]
        return remote(
            narrow.at[layer, 0, i], narrow.at[layer, 1, NARROW_Y.index(-d if d != 4 else 4)],
            r1_send.at[layer, len(WIDE_Y) + i], r1_recv.at[layer, 1], at(0, 0, core, d),
        )

    start_gather(0)
    loads[2].wait()
    lane = lax.broadcasted_iota(jnp.int32, (SLOTS, SLOTS), 1)
    slot = lax.broadcasted_iota(jnp.int32, (SLOTS, SLOTS), 0)
    place = coords[0:1, :] * (NX * NZ) + coords[1:2, :]
    place = jnp.where(lane[0:1] < count_ref[0, 0], place, -1)
    place = jnp.max(jnp.where(lane == slot, place, -1), axis=1, keepdims=True)
    hit = place == lax.broadcasted_iota(jnp.int32, (SLOTS, 2 * TILE), 1)
    used = jnp.where(hit, lax.broadcasted_iota(jnp.int32, (SLOTS, 2 * TILE), 0), SLOTS)
    table_v[...] = jnp.min(used, axis=0, keepdims=True)
    to_table = pltpu.make_async_copy(table_v, table, table_sem)
    to_table.start()
    tiles[SLOTS] = jnp.zeros((TILE, TILE), jnp.bfloat16)
    for load in loads[3:]:
        load.wait()
    to_table.wait()

    for layer in range(nl - 1):
        gather_multiply(layer)
        for i, d in enumerate(NARROW_Y):
            narrow[layer, 0, i] = acc[layer, (col + d + NY) % NY].astype(jnp.bfloat16)
            narrow_copy(layer, i).start()
        for i in range(len(WIDE_Y)):
            wide_copy(layer, i).start()
        total = acc[layer, col] + b1[...]
        if WIDE_Y:
            arrived(wide.at[layer], r1_recv.at[layer, 0])
            total += jnp.sum(wide[layer], axis=0)
        arrived(narrow.at[layer, 1], r1_recv.at[layer, 1])
        total += jnp.sum(narrow[layer, 1].astype(jnp.float32), axis=0)
        hidden = jnp.maximum(total, 0.0)
        zb[layer + 1, core, 0, 0] = jnp.dot(
            hidden, w2[...], precision=lax.Precision.HIGHEST, preferred_element_type=jnp.float32
        ).astype(jnp.bfloat16)
        start_gather(layer + 1)

    last = nl - 1
    gather_multiply(last)
    part2[...] = acc[last].astype(jnp.bfloat16)
    FAR_Y = (4, 3, -3, 2, -2, 1, -1)

    def r2_copy(i):
        d = FAR_Y[i]
        return remote(
            part2.at[(col + d + NY) % NY], back2.at[-d % NY - 1], r2_send.at[i], r2_recv, at(0, 0, core, d)
        )

    for i in range(len(FAR_Y)):
        r2_copy(i).start()

    for layer in range(nl - 1):
        for i in range(len(WIDE_Y)):
            wide_copy(layer, i).wait_send()
        for i in range(len(NARROW_Y)):
            narrow_copy(layer, i).wait_send()
    for layer in range(nl):
        drain(layer)

    own = acc[last, col] + b2[...]
    arrived(back2, r2_recv)
    out_ref[...] = own + jnp.sum(back2[...].astype(jnp.float32), axis=0)
    for i in range(len(FAR_Y)):
        r2_copy(i).wait_send()


def on_device(
    features, tile_coords, tile_count, tile_values, w_first, bias_first, w_second, bias_second, opt=OPT, cid=0, name=None
):
    hbm = pl.BlockSpec(memory_space=pltpu.HBM)
    dma = pltpu.SemaphoreType.DMA
    bf16, f32, i32 = jnp.bfloat16, jnp.float32, jnp.int32
    nl, nw, nn = opt["nl"], len(opt["WIDE_Y"]), len(opt["NARROW_Y"])
    in_hbm = (
        tile_coords[0, 0].T, features, tile_values[0, 0],
        w_first, bias_first.reshape(1, TILE), w_second, bias_second.reshape(1, TILE),
    )
    return pl.pallas_call(
        functools.partial(kernel, opt),
        name=name,
        out_shape=jax.ShapeDtypeStruct((NODE, TILE), f32),
        in_specs=[pl.BlockSpec(memory_space=pltpu.SMEM)] + [hbm] * 7,
        out_specs=pl.BlockSpec(memory_space=pltpu.VMEM),
        scratch_shapes=[
            pltpu.VMEM((2, SLOTS), i32),
            pltpu.VMEM((NODE, TILE), f32),
            pltpu.VMEM((SLOTS + 1, TILE, TILE), bf16),
            pltpu.VMEM((TILE, TILE), f32),
            pltpu.VMEM((1, TILE), f32),
            pltpu.VMEM((TILE, TILE), f32),
            pltpu.VMEM((1, TILE), f32),
            pltpu.VMEM((1, 2 * TILE), i32),
            pltpu.SMEM((1, 2 * TILE), i32),
            pltpu.VMEM((nl, 2, NZ, NX, NODE, TILE), bf16),
            pltpu.VMEM((nl, NY, NODE, TILE), f32),
            pltpu.VMEM((nl - 1, max(nw, 1), NODE, TILE), f32),
            pltpu.VMEM((nl - 1, 2, nn, NODE, TILE), bf16),
            pltpu.VMEM((NY, NODE, TILE), bf16),
            pltpu.VMEM((NY - 1, NODE, TILE), bf16),
            dma((7,)), dma,
            dma((nl, 11)), dma((nl, NZ)), dma((nl, 2)), dma((nl, NZ, 3)), dma((nl, NZ)), dma((nl, NZ)), dma((nl, NZ)),
            dma((nl - 1, 7)), dma((nl - 1, 2)), dma((7,)), dma,
        ],
        compiler_params=pltpu.CompilerParams(
            collective_id=cid, has_side_effects=True, vmem_limit_bytes=48 * 2**20
        ),
        cost_estimate=pl.CostEstimate(flops=3 * 10**9, bytes_accessed=2 * 10**6, transcendentals=0),
    )(tile_count, *[pltpu.with_memory_space_constraint(a, pltpu.HBM) for a in in_hbm])


def solution(mesh):
    return jax.shard_map(
        on_device,
        mesh=mesh,
        in_specs=(
            P(("row", "col"), None),
            P("row", "col", None, None),
            P("row", "col"),
            P("row", "col", None, None, None),
            P(),
            P(),
            P(),
            P(),
        ),
        out_specs=P(("row", "col"), None),
        check_vma=False,
    )
```

```python
import functools

import jax
import jax.numpy as jnp
from jax import lax
from jax.experimental import pallas as pl
from jax.experimental.pallas import tpu as pltpu
from jax.sharding import PartitionSpec as P

MESH = pl.DeviceIdType.MESH
NX, NZ, NY = 4, 12, 8
TILE, RT, SLOTS, NODE = 128, 4, 54, 64
OPT = dict(
    nl=2,
    SEND_Z=(2, -2, 3, -3, 4, -4, 5, -5, 6, 1, -1),
    BY_Z=(2, -2, 3, -3, 4, -4, 5, -5, 6),
    ZCOUNT=4,
    BUNDLES=((0,), (2,), (-2,), (3,), (-3,), (4,), (-4,), (1,), (-1,), (5,), (-5,), (6,)),
    LAG=6,
    X=(2, 1, -1),
    WIDE_Y=(), NARROW_Y=(4, 3, -3, 2, -2, 1, -1),
)


def kernel(
    opt,
    count_ref, coords_hbm, feat_hbm, tiles_hbm, w1_hbm, b1_hbm, w2_hbm, b2_hbm, out_ref,
    coords, feat, tiles, w1, b1, w2, b2, table_v, table, zb, acc, wide, narrow, part2, back2,
    load_sem, table_sem, z_send, z_recv, zx_send, x_send, x_recv, c_send, c_recv,
    r1_send, r1_recv, r2_send, r2_recv,
):
    nl, SEND_Z, BY_Z, BUNDLES, LAG, FAR_X = opt["nl"], opt["SEND_Z"], opt["BY_Z"], opt["BUNDLES"], opt["LAG"], opt["X"]
    WIDE_Y, NARROW_Y = opt["WIDE_Y"], opt["NARROW_Y"]
    NEAR_Z = (1, -1)
    order = [d for b in BUNDLES for d in b]
    rank = {d: k for k, d in enumerate(order)}
    rank[-6] = rank[6]
    row, col = lax.axis_index("row"), lax.axis_index("col")
    core = row % 2
    chip = row // 2
    z, x = chip % NZ, chip // NZ

    def at(dx, dz, c, dy=0):
        return (
            (((x + dx + NX) % NX) * NZ + (z + dz + NZ) % NZ) * 2 + c,
            (col + dy + NY) % NY,
        )

    def remote(src, dst, send, recv, to):
        return pltpu.make_async_remote_copy(
            src_ref=src, dst_ref=dst, send_sem=send, recv_sem=recv, device_id=to, device_id_type=MESH
        )

    sibling = at(0, 0, 1 - core)

    barrier = pltpu.get_barrier_semaphore()
    peers = [at(0, d, core) for d in (6, 5, -5, 4, -4)] + [at(0, 0, core, d) for d in (4, 3, -3)]
    peers += [at(0, d, core) for d in (3, -3, 2, -2, 1, -1)] + [at(0, 0, core, d) for d in (2, -2, 1, -1)]
    peers += [at(d, 0, core) for d in FAR_X] + [sibling]
    for to in peers:
        pl.semaphore_signal(barrier, inc=1, device_id=to, device_id_type=MESH)

    loads = [
        pltpu.make_async_copy(src, dst, load_sem.at[i])
        for i, (src, dst) in enumerate(
            (
                (feat_hbm, feat), (w1_hbm, w1), (coords_hbm, coords),
                (tiles_hbm, tiles.at[pl.ds(0, SLOTS)]), (b1_hbm, b1), (w2_hbm, w2), (b2_hbm, b2),
            )
        )
    ]
    for load in loads:
        load.start()

    loads[0].wait()
    loads[1].wait()
    zb[0, core, 0, 0] = jnp.dot(
        feat[...], w1[...], precision=lax.Precision.HIGHEST, preferred_element_type=jnp.float32
    ).astype(jnp.bfloat16)

    pl.semaphore_wait(barrier, len(peers))

    def z_copy(layer, i):
        d = SEND_Z[i]
        return remote(
            zb.at[layer, core, 0, 0], zb.at[layer, core, rank[-d], 0],
            z_send.at[layer, i], z_recv.at[layer, rank[-d]], at(0, d, core),
        )

    def x_copy(layer, dz, i):
        d, k = FAR_X[i], rank[dz]
        return remote(
            zb.at[layer, core, k, 0], zb.at[layer, core, k, -d % NX],
            x_send.at[layer, k, i], x_recv.at[layer, k], at(d, 0, core),
        )

    def pass_x_on(layer, i):
        d = NEAR_Z[i]
        return remote(
            zb.at[layer, core, 0, pl.ds(1, NX - 1)], zb.at[layer, core, rank[-d], pl.ds(1, NX - 1)],
            zx_send.at[layer, i], x_recv.at[layer, rank[-d]], at(0, d, core),
        )

    def c_copy(layer, b):
        first, size = rank[BUNDLES[b][0]], len(BUNDLES[b])
        block = zb.at[layer, core, pl.ds(first, size)]
        return remote(block, block, c_send.at[layer, b], c_recv.at[layer, b], sibling)

    def arrived(block, recv):
        remote(block, block, z_send.at[0, 0], recv, sibling).wait_recv()

    def multiply(layer, dz):
        za = (z + dz + NZ) % NZ
        places = [((x + dx) % NX) * NZ + za for dx in range(NX)]
        k = rank[dz]
        rhs = jnp.concatenate([zb[layer, c, k, dx] for dx in range(NX) for c in range(2)], axis=0)
        for r in range(RT):
            lhs = jnp.concatenate(
                [tiles[table[0, r * NX * NZ + p]] for p in places], axis=1
            )
            acc[layer, 2 * r : 2 * r + 2] += jnp.dot(
                lhs, rhs, preferred_element_type=jnp.float32
            ).reshape(2, NODE, TILE)

    def start_gather(layer):
        for i in range(len(FAR_X)):
            x_copy(layer, 0, i).start()
        for i in range(len(SEND_Z)):
            z_copy(layer, i).start()
        acc[layer] = jnp.zeros((NY, NODE, TILE), jnp.float32)

    def take_z(layer, dz):
        k = rank[dz]
        arrived(zb.at[layer, core, k, 0], z_recv.at[layer, k])
        if dz not in NEAR_Z:
            for i in range(len(FAR_X)):
                x_copy(layer, dz, i).start()

    def take_x(layer, dz):
        arrived(zb.at[layer, core, rank[dz], pl.ds(1, NX - 1)], x_recv.at[layer, rank[dz]])
        if dz == 0:
            for i in range(2):
                pass_x_on(layer, i).start()

    def gather_multiply(layer):
        for dz in BY_Z[: opt["ZCOUNT"]]:
            take_z(layer, dz)
        take_x(layer, 0)
        for dz in BY_Z[opt["ZCOUNT"] :] + NEAR_Z:
            take_z(layer, dz)
        for t in range(len(BUNDLES) + LAG):
            if t < len(BUNDLES):
                for dz in BUNDLES[t]:
                    if dz != 0:
                        take_x(layer, dz)
                c_copy(layer, t).start()
            if t >= LAG:
                b = t - LAG
                first, size = rank[BUNDLES[b][0]], len(BUNDLES[b])
                arrived(zb.at[layer, 1 - core, pl.ds(first, size)], c_recv.at[layer, b])
                for dz in BUNDLES[b]:
                    multiply(layer, dz)

    def drain(layer):
        for i in range(len(SEND_Z)):
            z_copy(layer, i).wait_send()
        for i in range(2):
            pass_x_on(layer, i).wait_send()
        for dz in order:
            for i in range(len(FAR_X) if dz not in NEAR_Z else 0):
                x_copy(layer, dz, i).wait_send()
        for b in range(len(BUNDLES)):
            c_copy(layer, b).wait_send()

    def wide_copy(layer, i):
        d = WIDE_Y[i]
        return remote(
            acc.at[layer, (col + d + NY) % NY], wide.at[layer, WIDE_Y.index(-d)],
            r1_send.at[layer, i], r1_recv.at[layer, 0], at(0, 0, core, d),
        )

    def narrow_copy(layer, i):
        d = NARROW_Y[i]
        return remote(
            narrow.at[layer, 0, i], narrow.at[layer, 1, NARROW_Y.index(-d if d != 4 else 4)],
            r1_send.at[layer, len(WIDE_Y) + i], r1_recv.at[layer, 1], at(0, 0, core, d),
        )

    def settle(layer):
        for i in range(len(WIDE_Y)):
            wide_copy(layer, i).wait_send()
        for i in range(len(NARROW_Y)):
            narrow_copy(layer, i).wait_send()
        drain(layer)

    start_gather(0)
    loads[2].wait()
    lane = lax.broadcasted_iota(jnp.int32, (SLOTS, SLOTS), 1)
    slot = lax.broadcasted_iota(jnp.int32, (SLOTS, SLOTS), 0)
    place = coords[0:1, :] * (NX * NZ) + coords[1:2, :]
    place = jnp.where(lane[0:1] < count_ref[0, 0], place, -1)
    place = jnp.max(jnp.where(lane == slot, place, -1), axis=1, keepdims=True)
    hit = place == lax.broadcasted_iota(jnp.int32, (SLOTS, 2 * TILE), 1)
    used = jnp.where(hit, lax.broadcasted_iota(jnp.int32, (SLOTS, 2 * TILE), 0), SLOTS)
    table_v[...] = jnp.min(used, axis=0, keepdims=True)
    to_table = pltpu.make_async_copy(table_v, table, table_sem)
    to_table.start()
    tiles[SLOTS] = jnp.zeros((TILE, TILE), jnp.bfloat16)
    for load in loads[3:]:
        load.wait()
    to_table.wait()

    for layer in range(nl - 1):
        gather_multiply(layer)
        for i, d in enumerate(NARROW_Y):
            narrow[layer, 0, i] = acc[layer, (col + d + NY) % NY].astype(jnp.bfloat16)
            narrow_copy(layer, i).start()
        for i in range(len(WIDE_Y)):
            wide_copy(layer, i).start()
        total = acc[layer, col] + b1[...]
        if WIDE_Y:
            arrived(wide.at[layer], r1_recv.at[layer, 0])
            total += jnp.sum(wide[layer], axis=0)
        arrived(narrow.at[layer, 1], r1_recv.at[layer, 1])
        total += jnp.sum(narrow[layer, 1].astype(jnp.float32), axis=0)
        hidden = jnp.maximum(total, 0.0)
        zb[layer + 1, core, 0, 0] = jnp.dot(
            hidden, w2[...], precision=lax.Precision.HIGHEST, preferred_element_type=jnp.float32
        ).astype(jnp.bfloat16)
        start_gather(layer + 1)
        settle(layer)

    last = nl - 1
    gather_multiply(last)
    part2[...] = acc[last].astype(jnp.bfloat16)
    FAR_Y = (4, 3, -3, 2, -2, 1, -1)

    def r2_copy(i):
        d = FAR_Y[i]
        return remote(
            part2.at[(col + d + NY) % NY], back2.at[-d % NY - 1], r2_send.at[i], r2_recv, at(0, 0, core, d)
        )

    for i in range(len(FAR_Y)):
        r2_copy(i).start()

    drain(last)

    own = acc[last, col] + b2[...]
    arrived(back2, r2_recv)
    out_ref[...] = own + jnp.sum(back2[...].astype(jnp.float32), axis=0)
    for i in range(len(FAR_Y)):
        r2_copy(i).wait_send()


def on_device(
    features, tile_coords, tile_count, tile_values, w_first, bias_first, w_second, bias_second, opt=OPT, cid=0, name=None
):
    hbm = pl.BlockSpec(memory_space=pltpu.HBM)
    dma = pltpu.SemaphoreType.DMA
    bf16, f32, i32 = jnp.bfloat16, jnp.float32, jnp.int32
    nl, nw, nn = opt["nl"], len(opt["WIDE_Y"]), len(opt["NARROW_Y"])
    in_hbm = (
        tile_coords[0, 0].T, features, tile_values[0, 0],
        w_first, bias_first.reshape(1, TILE), w_second, bias_second.reshape(1, TILE),
    )
    return pl.pallas_call(
        functools.partial(kernel, opt),
        name=name,
        out_shape=jax.ShapeDtypeStruct((NODE, TILE), f32),
        in_specs=[pl.BlockSpec(memory_space=pltpu.SMEM)] + [hbm] * 7,
        out_specs=pl.BlockSpec(memory_space=pltpu.VMEM),
        scratch_shapes=[
            pltpu.VMEM((2, SLOTS), i32),
            pltpu.VMEM((NODE, TILE), f32),
            pltpu.VMEM((SLOTS + 1, TILE, TILE), bf16),
            pltpu.VMEM((TILE, TILE), f32),
            pltpu.VMEM((1, TILE), f32),
            pltpu.VMEM((TILE, TILE), f32),
            pltpu.VMEM((1, TILE), f32),
            pltpu.VMEM((1, 2 * TILE), i32),
            pltpu.SMEM((1, 2 * TILE), i32),
            pltpu.VMEM((nl, 2, NZ, NX, NODE, TILE), bf16),
            pltpu.VMEM((nl, NY, NODE, TILE), f32),
            pltpu.VMEM((nl - 1, max(nw, 1), NODE, TILE), f32),
            pltpu.VMEM((nl - 1, 2, nn, NODE, TILE), bf16),
            pltpu.VMEM((NY, NODE, TILE), bf16),
            pltpu.VMEM((NY - 1, NODE, TILE), bf16),
            dma((7,)), dma,
            dma((nl, 11)), dma((nl, NZ)), dma((nl, 2)), dma((nl, NZ, 3)), dma((nl, NZ)), dma((nl, NZ)), dma((nl, NZ)),
            dma((nl - 1, 7)), dma((nl - 1, 2)), dma((7,)), dma,
        ],
        compiler_params=pltpu.CompilerParams(
            collective_id=cid, has_side_effects=True, vmem_limit_bytes=48 * 2**20
        ),
        cost_estimate=pl.CostEstimate(flops=3 * 10**9, bytes_accessed=2 * 10**6, transcendentals=0),
    )(tile_count, *[pltpu.with_memory_space_constraint(a, pltpu.HBM) for a in in_hbm])


def solution(mesh):
    return jax.shard_map(
        on_device,
        mesh=mesh,
        in_specs=(
            P(("row", "col"), None),
            P("row", "col", None, None),
            P("row", "col"),
            P("row", "col", None, None, None),
            P(),
            P(),
            P(),
            P(),
        ),
        out_specs=P(("row", "col"), None),
        check_vma=False,
    )
```
